128 devices in a mesh: dp: 32 (over y, z, core), tensor: 4 (over x).
Axes of the slice: x: 4, y: 4, z: 4, core: 2. Of those that a mesh axis runs over, the one named last changes fastest.
Arguments:
- queries: bfloat16 [4096, 4096], P('dp', 'tensor'), may hold values from -120 to 120
- token_keys: bfloat16 [4096, 512], P('dp', 'tensor'), may hold values from -4 to 4
- token_values: bfloat16 [4096, 512], P('dp', 'tensor'), may hold values from -4 to 4
- cached_key_rows: bfloat16 [4096, 256, 512], P('dp', None, 'tensor'), may hold values from -4 to 4
- cached_value_rows: bfloat16 [4096, 256, 512], P('dp', None, 'tensor'), may hold values from -4 to 4
- cache_length: int32 [4096], P('dp'), may hold values from 2 to 256, as said below
- output_projection: bfloat16 [4096, 8192], P(None, 'tensor'), may hold values from -0.75 to 0.75
- request_adapter: int32 [4096], P('dp'), may hold values from 0 to 31, as said below
- adapter_table_row: int32 [32], replicated, may hold values from 0 to 31, each once
- adapter_down_weight: bfloat16 [32, 64, 4096], P('dp', None, 'tensor'), may hold values from -0.75 to 0.75
- adapter_up_weight: bfloat16 [32, 64, 8192], P('dp', None, 'tensor'), may hold values from -0.75 to 0.75
Outputs:
- mixed: bfloat16 [4096, 8192], P('dp', 'tensor')
The draws below stay inside these ranges and needn't reach their ends.
Inputs may be any that keep to these rules, and one draw needn't show every extreme that they name: `cache_length`: at least one request has exactly 256 used positions. `request_adapter`: among the 128 requests of one index of dp no adapter id occurs more than 8 times; in every draw one adapter id occurs exactly 8 times on every index of dp. `adapter_table_row`: each row 0 to 31 is named once.
All inputs are finite; a program needn't handle non-finite values.
Results may differ from the reference program's by a relative error of at most 0.01.
Values may be sent and summed in bfloat16 or wider, within the bound.
No kernel may reach another device: no remote copies, remote signals or barrier semaphores. Data moves between devices by JAX's collectives and lax.ppermute only.
A program may use at most 128 MiB of HBM per device.

```python
import math
import jax
import jax.numpy as jnp
from jax import lax

MODEL_WIDTH = 8192
HEADS = 32
KV_HEADS = 4
HEAD_DIM = 128
ADAPTER_RANK = 64
R_DEV = 128
CACHE = 256
ADAPTER_COUNT = 32
CAP = 8
REQUESTS = 4096
QUERY_FEATURES = 4096
KV_WIDTH = 512


def joint_draw(key):
    key_part = jnp.clip(jax.random.normal(jax.random.fold_in(key, 1), (REQUESTS, CACHE, KV_WIDTH), jnp.float32), -4.0, 4.0)
    query_part = jnp.clip(jax.random.normal(jax.random.fold_in(key, 2), (REQUESTS, QUERY_FEATURES), jnp.float32), -4.0, 4.0)
    return (query_part, key_part)


def draw_queries(key, part):
    return joint_draw(key)[0].astype(jnp.bfloat16)


def draw_cached_key_rows(key, part):
    return joint_draw(key)[1].astype(jnp.bfloat16)


def draw_cache_length(key, part):
    blocks = REQUESTS // R_DEV
    ceiling = jax.random.randint(jax.random.fold_in(key, 11), (blocks, 1), 2, CACHE + 1)
    lengths = jax.random.randint(jax.random.fold_in(key, 12), (blocks, R_DEV), 2, ceiling + 1).reshape(REQUESTS)
    longest = jax.random.randint(jax.random.fold_in(key, 13), (), 0, REQUESTS)
    lengths = jnp.where(jnp.arange(REQUESTS, dtype=jnp.int32) == longest, CACHE, lengths)
    return lengths.astype(jnp.int32)


def draw_request_adapter(key, part):
    blocks = REQUESTS // R_DEV
    adapter_copies = ADAPTER_COUNT * CAP
    adapter_popularity = jax.random.randint(jax.random.fold_in(key, 21), (ADAPTER_COUNT,), 0, 4)
    favoured_adapters = jax.random.randint(jax.random.fold_in(key, 22), (), 0, ADAPTER_COUNT)
    copy_order = jnp.arange(adapter_copies, dtype=jnp.int32)
    copy_holder = copy_order // CAP
    first_copy = copy_order % CAP == 0
    end_holder = (copy_holder == 0) | (copy_holder == ADAPTER_COUNT - 1)
    top_level = (copy_holder == favoured_adapters) | first_copy & end_holder
    extra_weight = adapter_popularity[copy_holder] * 32768 + jnp.where(top_level, 2097152, 0)

    def one_block(block_index):
        block_key = jax.random.fold_in(key, 100 + block_index)
        random_noise = jax.random.randint(jax.random.fold_in(block_key, 1), (adapter_copies,), 0, 65536)
        attention_scores = (extra_weight + random_noise) * adapter_copies + copy_order
        values_top, picked = lax.top_k(attention_scores, R_DEV)
        adapters_picked = picked // CAP
        shuffle = jax.random.permutation(jax.random.fold_in(block_key, 2), R_DEV)
        return adapters_picked[shuffle]
    return jax.vmap(one_block)(jnp.arange(blocks, dtype=jnp.int32)).reshape(REQUESTS).astype(jnp.int32)


def steps_of(stream_key, shape, split, smallest, top_value):
    loudness, own = 1.0, jax.random.fold_in(stream_key, 6)
    for axis_at, shards_of in split:
        heights = jnp.exp(jax.random.uniform(jax.random.fold_in(own, axis_at), (shards_of,), jnp.float32, smallest / len(split), top_value / len(split)))
        loudness = loudness * jnp.repeat(heights, shape[axis_at] // shards_of).reshape([-1 if axis == axis_at else 1 for axis in range(len(shape))])
    return loudness


def gaussian(rng, shape, scale, reach, cuts=(), held_as=jnp.bfloat16):
    gain = steps_of(rng, shape, cuts, -0.22, 0.18) if cuts else 1.0
    drawn = jax.random.normal(rng, shape, jnp.float32) * scale * gain
    return jnp.minimum(jnp.maximum(drawn, -reach), reach).astype(held_as)


def setup_inputs(seed: int = 0) -> dict:
    streams_of = jax.random.split(jax.random.key(seed), 12)
    queries = draw_queries(jax.random.fold_in(streams_of[11], 71), 0)
    token_keys = gaussian(streams_of[1], (REQUESTS, KV_WIDTH), 1.0, 4.0, ((0, 32), (1, 4)))
    token_values = gaussian(streams_of[2], (REQUESTS, KV_WIDTH), 1.0, 4.0, ((0, 32), (1, 4)))
    cached_key_rows = draw_cached_key_rows(jax.random.fold_in(streams_of[11], 71), 0)
    cached_value_rows = gaussian(streams_of[4], (REQUESTS, CACHE, KV_WIDTH), 1.0, 4.0, ((0, 32), (2, 4)))
    cache_length = draw_cache_length(jax.random.fold_in(streams_of[11], 71), 0)
    output_projection = gaussian(streams_of[6], (QUERY_FEATURES, MODEL_WIDTH), (QUERY_FEATURES // 64) ** -0.5, 0.75, ((1, 4),))
    request_adapter = draw_request_adapter(jax.random.fold_in(streams_of[11], 71), 0)
    adapter_table_row = jax.random.permutation(streams_of[8], ADAPTER_COUNT).astype(jnp.int32)
    adapter_down_weight = gaussian(streams_of[9], (ADAPTER_COUNT, ADAPTER_RANK, QUERY_FEATURES), (QUERY_FEATURES // 64) ** -0.5, 0.75, ((0, 32), (2, 4)))
    adapter_up_weight = gaussian(streams_of[10], (ADAPTER_COUNT, ADAPTER_RANK, MODEL_WIDTH), ADAPTER_RANK ** -0.5, 0.75, ((0, 32), (2, 4)))
    return dict(queries=queries, token_keys=token_keys, token_values=token_values, cached_key_rows=cached_key_rows, cached_value_rows=cached_value_rows, cache_length=cache_length, output_projection=output_projection, request_adapter=request_adapter, adapter_table_row=adapter_table_row, adapter_down_weight=adapter_down_weight, adapter_up_weight=adapter_up_weight)


def attend_block(arrays):
    queries, token_keys, token_values, cached_key_rows, cached_value_rows, cache_length = arrays
    requests = queries.shape[0]
    per_group = HEADS // KV_HEADS
    highest = lax.Precision.HIGHEST
    score_scale = 1.0 / math.sqrt(HEAD_DIM)
    query_heads = queries.astype(jnp.float32).reshape(requests, KV_HEADS, per_group, HEAD_DIM)
    key_blocks = cached_key_rows.astype(jnp.float32).reshape(requests, CACHE, KV_HEADS, HEAD_DIM)
    value_blocks = cached_value_rows.astype(jnp.float32).reshape(requests, CACHE, KV_HEADS, HEAD_DIM)
    fresh_keys = token_keys.astype(jnp.float32).reshape(requests, KV_HEADS, HEAD_DIM)
    fresh_values = token_values.astype(jnp.float32).reshape(requests, KV_HEADS, HEAD_DIM)
    cached_score = jnp.einsum('rkgd,rpkd->rkgp', query_heads, key_blocks, precision=highest) * score_scale
    fresh_score = jnp.einsum('rkgd,rkd->rkg', query_heads, fresh_keys, precision=highest) * score_scale
    in_cache = (jnp.arange(CACHE, dtype=jnp.int32)[None, :] < cache_length[:, None])[:, None, None, :]
    row_max = jnp.maximum(lax.optimization_barrier(jnp.max(jnp.where(in_cache, cached_score, -jnp.inf), axis=-1)), fresh_score)
    cached_weight = jnp.where(in_cache, jnp.exp(cached_score - row_max[..., None]), 0.0)
    fresh_weight = jnp.exp(fresh_score - row_max)
    weight_sum = lax.optimization_barrier(jnp.sum(cached_weight, axis=-1)) + fresh_weight
    cached_round = lax.optimization_barrier(cached_weight.astype(jnp.bfloat16)).astype(jnp.float32)
    fresh_round = lax.optimization_barrier(fresh_weight.astype(jnp.bfloat16)).astype(jnp.float32)
    combined = jnp.einsum('rkgp,rpkd->rkgd', cached_round, value_blocks, precision=highest)
    combined = combined + fresh_round[..., None] * fresh_values[:, :, None, :]
    return (combined / weight_sum[..., None]).reshape(requests, HEADS * HEAD_DIM).astype(jnp.bfloat16)

def reference(queries, token_keys, token_values, cached_key_rows, cached_value_rows, cache_length, output_projection, request_adapter, adapter_table_row, adapter_down_weight, adapter_up_weight):
    blocks = REQUESTS // R_DEV
    arrays = (queries, token_keys, token_values, cached_key_rows, cached_value_rows, cache_length)
    blocked = tuple((item.reshape((blocks, R_DEV) + item.shape[1:]) for item in arrays))
    attention_output = lax.map(attend_block, blocked).reshape(REQUESTS, HEADS * HEAD_DIM)
    slot_of = adapter_table_row[request_adapter]
    adapter_range = jnp.arange(ADAPTER_COUNT, dtype=jnp.int32)

    def add_low(carried, table_row_index):
        rank_products = jnp.dot(attention_output, adapter_down_weight[table_row_index].T, preferred_element_type=jnp.float32)
        return (jnp.where((slot_of == table_row_index)[:, None], rank_products, carried), None)
    low_rank_state, unused = lax.scan(add_low, jnp.zeros((REQUESTS, ADAPTER_RANK), jnp.float32), adapter_range)
    low_rank_state = low_rank_state.astype(jnp.bfloat16)

    def add_delta(carried, table_row_index):
        rank_products = jnp.dot(low_rank_state, adapter_up_weight[table_row_index], preferred_element_type=jnp.float32).astype(jnp.bfloat16)
        return (jnp.where((slot_of == table_row_index)[:, None], rank_products, carried), None)
    adapter_deltas, unused_too = lax.scan(add_delta, jnp.zeros((REQUESTS, MODEL_WIDTH), jnp.bfloat16), adapter_range)
    projected = jnp.dot(attention_output, output_projection, preferred_element_type=jnp.float32)
    return (projected + adapter_deltas.astype(jnp.float32)).astype(jnp.bfloat16)
```

```python
import math

import jax
import jax.numpy as jnp
from jax import lax
from jax.sharding import PartitionSpec as P

HEADS = 32
KV_HEADS = 4
HEAD_DIM = 128
CAP = 8
Z_CHIPS = 4
CORES = 2
RING = 4


def attend(queries, token_keys, token_values, cached_key_rows, cached_value_rows, cache_length):
    requests = queries.shape[0]
    per_group = HEADS // KV_HEADS
    positions = cached_key_rows.shape[1]
    score_scale = 1.0 / math.sqrt(HEAD_DIM)
    query_heads = queries.reshape(requests, per_group, HEAD_DIM)
    cached_score = (
        jnp.einsum("rgd,rpd->rgp", query_heads, cached_key_rows, preferred_element_type=jnp.float32)
        * score_scale
    )
    fresh_score = (
        jnp.einsum("rgd,rd->rg", query_heads, token_keys, preferred_element_type=jnp.float32)
        * score_scale
    )
    in_cache = (jnp.arange(positions, dtype=jnp.int32)[None, :] < cache_length[:, None])[:, None, :]
    row_max = jnp.maximum(
        jnp.max(jnp.where(in_cache, cached_score, -jnp.inf), axis=-1), fresh_score
    )
    cached_weight = jnp.where(in_cache, jnp.exp(cached_score - row_max[..., None]), 0.0)
    fresh_weight = jnp.exp(fresh_score - row_max)
    weight_sum = jnp.sum(cached_weight, axis=-1) + fresh_weight
    combined = jnp.einsum(
        "rgp,rpd->rgd",
        cached_weight.astype(jnp.bfloat16),
        cached_value_rows,
        preferred_element_type=jnp.float32,
    )
    combined = combined + jnp.einsum(
        "rg,rd->rgd",
        fresh_weight.astype(jnp.bfloat16),
        token_values,
        preferred_element_type=jnp.float32,
    )
    return (
        (combined / weight_sum[..., None])
        .reshape(requests, per_group * HEAD_DIM)
        .astype(jnp.bfloat16)
    )


def swap_tensor(value, k):
    return lax.ppermute(value, "tensor", [(i, i ^ k) for i in range(RING)])


def swap_dp(value, k):
    return lax.ppermute(value, "dp", [(i, i ^ k) for i in range(RING * Z_CHIPS * CORES)])


def on_device(
    queries,
    token_keys,
    token_values,
    cached_key_rows,
    cached_value_rows,
    cache_length,
    output_projection,
    request_adapter,
    adapter_table_row,
    adapter_down_weight,
    adapter_up_weight,
):
    bf16, f32 = jnp.bfloat16, jnp.float32
    requests = queries.shape[0]
    features = queries.shape[1]
    rank = adapter_down_weight.shape[1]
    columns = output_projection.shape[1]
    owned = Z_CHIPS * CORES
    here = lax.axis_index("dp")
    mine = lax.axis_index("tensor")

    weights = jnp.concatenate([adapter_down_weight[0], adapter_up_weight[0]], axis=1)
    over_z = jnp.stack([weights] + [swap_dp(weights, k * CORES) for k in range(1, Z_CHIPS)])
    table = jnp.stack([over_z, swap_dp(over_z, 1)], axis=1).reshape(owned, rank, features + columns)
    table_down, table_up = table[:, :, :features], table[:, :, features:]

    attended = attend(
        queries, token_keys, token_values, cached_key_rows, cached_value_rows, cache_length
    )

    every_adapter = adapter_table_row.shape[0]
    matches = request_adapter[:, None] == jnp.arange(every_adapter, dtype=jnp.int32)[None, :]
    slot_of = jnp.sum(jnp.where(matches, adapter_table_row[None, :], 0), axis=1)
    order = jnp.arange(requests, dtype=jnp.int32)
    earlier = (slot_of[:, None] == slot_of[None, :]) & (order[:, None] > order[None, :])
    position = (slot_of ^ here) * CAP + jnp.sum(earlier.astype(jnp.int32), axis=1)
    placing = (
        jnp.arange(every_adapter * CAP, dtype=jnp.int32)[:, None] == position[None, :]
    ).astype(bf16)
    placed = jnp.dot(placing, attended, preferred_element_type=f32).astype(bf16)
    placed = placed.reshape(RING, owned * CAP, features)
    routed = [placed[0]] + [swap_dp(placed[m], m * owned) for m in range(1, RING)]

    pieces = [attended] + [swap_tensor(attended, k) for k in range(1, RING)]
    gathered = jnp.zeros((requests, RING * features), bf16)
    for k, piece in enumerate(pieces):
        gathered = lax.dynamic_update_slice(gathered, piece, (0, (mine ^ k) * features))
    projected = jnp.dot(gathered, output_projection, preferred_element_type=f32)

    grouped = jnp.stack(routed).reshape(RING, owned, CAP, features)
    partial = jnp.einsum("makw,arw->amkr", grouped, table_down, preferred_element_type=f32)
    partial = partial.reshape(2, owned * RING * CAP // 2, rank)
    partial = jnp.concatenate([partial[0], partial[1]], axis=1)
    total = partial
    for k in range(1, RING):
        total = total + swap_tensor(partial, k)
    low_rank = total.astype(bf16)
    low_rank = jnp.stack([low_rank[:, :rank], low_rank[:, rank:]]).reshape(owned, RING, CAP, rank)
    delta = jnp.einsum("amkr,ard->makd", low_rank, table_up, preferred_element_type=f32).astype(
        bf16
    )
    delta = delta.reshape(RING, owned * CAP, columns)
    back = [delta[0]] + [swap_dp(delta[m], m * owned) for m in range(1, RING)]
    returned = jnp.dot(placing.T, jnp.concatenate(back, axis=0), preferred_element_type=f32)
    return (projected + returned).astype(bf16)


def solution(mesh):
    in_specs = (
        P("dp", "tensor"),
        P("dp", "tensor"),
        P("dp", "tensor"),
        P("dp", None, "tensor"),
        P("dp", None, "tensor"),
        P("dp"),
        P(None, "tensor"),
        P("dp"),
        P(),
        P("dp", None, "tensor"),
        P("dp", None, "tensor"),
    )
    out_specs = P("dp", "tensor")
    return jax.shard_map(
        on_device, mesh=mesh, in_specs=in_specs, out_specs=out_specs, check_vma=False
    )
```

```python
import functools
import math

import jax
import jax.numpy as jnp
from jax import lax
from jax.experimental import pallas as pl
from jax.experimental.pallas import tpu as pltpu
from jax.sharding import PartitionSpec as P

HEADS = 32
KV_HEADS = 4
HEAD_DIM = 128
CAP = 8
Z_CHIPS = 4
CORES = 2
RING = 4
GROUP = HEADS // KV_HEADS
BLOCK = 32
ATTEND_VMEM = 63 * 2**20
STAGED = 6
DEPTH = 512


def slot_positions(request_adapter, table_ref):
    i32, f32 = jnp.int32, jnp.float32
    requests = request_adapter.shape[1]
    slot = jnp.zeros_like(request_adapter)
    for adapter in range(table_ref.shape[0]):
        slot = jnp.where(request_adapter == adapter, table_ref[adapter], slot)
    square = (requests, requests)
    across = jnp.broadcast_to(slot.astype(f32), square)
    earlier = (across.T == across) & (
        lax.broadcasted_iota(i32, square, 0) < lax.broadcasted_iota(i32, square, 1)
    )
    count = jnp.sum(jnp.where(earlier, 1.0, 0.0), axis=0, keepdims=True).astype(i32)
    return (slot ^ lax.axis_index("dp")) * CAP + count


def attend_kernel(*refs):
    sources, (key_hbm, value_hbm), refs = refs[:STAGED], refs[STAGED : STAGED + 2], refs[STAGED + 2 :]
    attended_ref, bucket_refs, refs = refs[0], refs[1 : 1 + RING], refs[1 + RING :]
    staged, refs = refs[:STAGED], refs[STAGED:]
    length_ref, table_ref, adapter_ref, query_ref, token_key_ref, token_value_ref = staged
    key_ref, value_ref, heads_ref, fresh_key_ref, fresh_value_ref, mixed_ref, used_ref = refs[:7]
    staged_sem, key_sem, value_sem = refs[7:]
    f32, bf16 = jnp.float32, jnp.bfloat16
    requests, positions, _ = key_ref.shape
    score_scale = 1.0 / math.sqrt(HEAD_DIM)

    def fetch(source, target, sem, c):
        at = pl.ds(c * BLOCK, BLOCK)
        return pltpu.make_async_copy(source.at[at], target.at[at], sem.at[c])

    staging = [
        pltpu.make_async_copy(source, target, staged_sem.at[i])
        for i, (source, target) in enumerate(zip(sources, staged))
    ]
    for copy in staging:
        copy.start()
    for c in range(requests // BLOCK):
        fetch(key_hbm, key_ref, key_sem, c).start()
        fetch(value_hbm, value_ref, value_sem, c).start()
    for copy in staging:
        copy.wait()
    slots_at = slot_positions(adapter_ref[...], table_ref)

    for c in range(requests // BLOCK):
        rows = slice(c * BLOCK, (c + 1) * BLOCK)
        fresh_keys = token_key_ref[rows, :].astype(f32)
        fresh_values = token_value_ref[rows, :].astype(f32)
        for h in range(GROUP):
            at = pl.ds(h, BLOCK, stride=GROUP)
            heads_ref[at, :] = query_ref[rows, h * HEAD_DIM : (h + 1) * HEAD_DIM].astype(f32)
            fresh_key_ref[at, :] = fresh_keys
            fresh_value_ref[at, :] = fresh_values
        for r in range(BLOCK):
            used_ref[r * GROUP : (r + 1) * GROUP, :] = jnp.full(
                (GROUP, positions), length_ref[c * BLOCK + r], jnp.int32
            )
        heads = heads_ref[...]
        fetch(key_hbm, key_ref, key_sem, c).wait()
        score = lax.dot_general(
            heads.reshape(BLOCK, GROUP, HEAD_DIM).astype(bf16),
            key_ref[rows],
            (((2,), (2,)), ((0,), (0,))),
            preferred_element_type=f32,
        )
        score = score.reshape(BLOCK * GROUP, positions) * score_scale
        fresh = jnp.sum(heads * fresh_key_ref[...], axis=1, keepdims=True) * score_scale
        place = lax.broadcasted_iota(jnp.int32, score.shape, 1)
        score = jnp.where(place < used_ref[...], score, -jnp.inf)
        row_max = jnp.maximum(jnp.max(score, axis=1, keepdims=True), fresh)
        weight = jnp.exp(score - row_max)
        fresh_weight = jnp.exp(fresh - row_max)
        weight_sum = jnp.sum(weight, axis=1, keepdims=True) + fresh_weight
        fetch(value_hbm, value_ref, value_sem, c).wait()
        mixed = lax.dot_general(
            weight.reshape(BLOCK, GROUP, positions).astype(bf16),
            value_ref[rows],
            (((2,), (1,)), ((0,), (0,))),
            preferred_element_type=f32,
        ).reshape(BLOCK * GROUP, HEAD_DIM)
        mixed = mixed + fresh_weight.astype(bf16).astype(f32) * fresh_value_ref[...]
        mixed_ref[...] = mixed / weight_sum
        for h in range(GROUP):
            attended_ref[0, rows, h * HEAD_DIM : (h + 1) * HEAD_DIM] = mixed_ref[
                pl.ds(h, BLOCK, stride=GROUP), :
            ].astype(bf16)

    attended = attended_ref[0]
    for k in range(1, RING):
        attended_ref[k] = attended
    for m, bucket_ref in enumerate(bucket_refs):
        slots = bucket_ref.shape[0]
        wanted = m * slots + lax.broadcasted_iota(jnp.int32, (slots, requests), 0)
        placing = jnp.where(wanted == slots_at, 1.0, 0.0).astype(bf16)
        bucket_ref[...] = jnp.dot(placing, attended, preferred_element_type=f32).astype(bf16)


def attend(
    queries,
    token_keys,
    token_values,
    cached_key_rows,
    cached_value_rows,
    cache_length,
    request_adapter,
    adapter_table_row,
    slots,
):
    requests, features = queries.shape
    positions = cached_key_rows.shape[1]
    vmem = pl.BlockSpec(memory_space=pltpu.VMEM)
    hbm = pl.BlockSpec(memory_space=pltpu.HBM)
    per_head = pltpu.VMEM((BLOCK * GROUP, HEAD_DIM), jnp.float32)
    fetches = pltpu.SemaphoreType.DMA((requests // BLOCK,))
    return pl.pallas_call(
        attend_kernel,
        in_specs=[hbm] * (STAGED + 2),
        out_specs=[vmem] * (1 + RING),
        out_shape=[jax.ShapeDtypeStruct((RING, requests, features), jnp.bfloat16)]
        + [jax.ShapeDtypeStruct((slots, features), jnp.bfloat16)] * RING,
        scratch_shapes=[
            pltpu.SMEM(cache_length.shape, jnp.int32),
            pltpu.SMEM(adapter_table_row.shape, jnp.int32),
            pltpu.VMEM((1, requests), jnp.int32),
            pltpu.VMEM(queries.shape, jnp.bfloat16),
            pltpu.VMEM(token_keys.shape, jnp.bfloat16),
            pltpu.VMEM(token_values.shape, jnp.bfloat16),
        ]
        + [pltpu.VMEM(cached_key_rows.shape, jnp.bfloat16)] * 2
        + [per_head] * 4
        + [pltpu.VMEM((BLOCK * GROUP, positions), jnp.int32)]
        + [pltpu.SemaphoreType.DMA((STAGED,)), fetches, fetches],
        compiler_params=pltpu.CompilerParams(vmem_limit_bytes=ATTEND_VMEM),
        cost_estimate=pl.CostEstimate(
            flops=4 * requests * GROUP * positions * HEAD_DIM,
            bytes_accessed=4 * requests * positions * HEAD_DIM,
            transcendentals=requests * GROUP * positions,
        ),
    )(
        cache_length,
        adapter_table_row,
        request_adapter.reshape(1, requests),
        queries,
        token_keys,
        token_values,
        cached_key_rows,
        cached_value_rows,
    )


def down_kernel(*refs):
    routed, weights, out_ref = refs[:RING], refs[RING:-1], refs[-1]
    rank = weights[0].shape[0]
    features = routed[0].shape[1]
    pair = CORES * CAP
    for k in range(Z_CHIPS):
        rows = jnp.concatenate([r[k * pair : (k + 1) * pair, :] for r in routed], axis=0)
        products = [
            lax.dot_general(
                rows,
                w[:, :features],
                (((1,), (1,)), ((), ())),
                preferred_element_type=jnp.float32,
            )
            for w in weights[k * CORES : (k + 1) * CORES]
        ]
        for m in range(RING):
            at = (k * RING + m) * CAP
            for j, product in enumerate(products):
                row = m * pair + j * CAP
                out_ref[at : at + CAP, j * rank : (j + 1) * rank] = product[row : row + CAP, :]


def down(routed, weights):
    rank = weights[0].shape[0]
    vmem = pl.BlockSpec(memory_space=pltpu.VMEM)
    return pl.pallas_call(
        down_kernel,
        in_specs=[vmem] * (len(routed) + len(weights)),
        out_specs=vmem,
        out_shape=jax.ShapeDtypeStruct((Z_CHIPS * RING * CAP, CORES * rank), jnp.float32),
        compiler_params=pltpu.CompilerParams(vmem_limit_bytes=16 * 2**20),
    )(*routed, *weights)


def up_kernel(columns, *refs):
    partials, weights, deltas = refs[:RING], refs[RING:-RING], refs[-RING:]
    rank = weights[0].shape[0]
    pair = CORES * CAP
    total = partials[0][...] + partials[1][...] + partials[2][...] + partials[3][...]
    for k in range(Z_CHIPS):
        part = total[k * RING * CAP : (k + 1) * RING * CAP, :]
        spread = []
        for m in range(RING):
            spread += [part[m * CAP : (m + 1) * CAP, :]] * CORES
        spread = jnp.concatenate(spread, axis=0)
        row = lax.broadcasted_iota(jnp.int32, spread.shape, 0)
        lane = lax.broadcasted_iota(jnp.int32, spread.shape, 1)
        low_rank = jnp.where((row // CAP) % CORES == lane // rank, spread, 0.0)
        low_rank = low_rank.astype(jnp.bfloat16)
        delta = 0.0
        for j, w in enumerate(weights[k * CORES : (k + 1) * CORES]):
            delta += jnp.dot(
                low_rank[:, j * rank : (j + 1) * rank],
                w[:, w.shape[1] - columns :],
                preferred_element_type=jnp.float32,
            )
        delta = delta.astype(jnp.bfloat16)
        for m, delta_ref in enumerate(deltas):
            delta_ref[k * pair : (k + 1) * pair, :] = delta[m * pair : (m + 1) * pair, :]


def up(partials, weights, columns):
    rows = Z_CHIPS * CORES * CAP
    vmem = pl.BlockSpec(memory_space=pltpu.VMEM)
    return pl.pallas_call(
        functools.partial(up_kernel, columns),
        in_specs=[vmem] * (len(partials) + len(weights)),
        out_specs=[vmem] * RING,
        out_shape=[jax.ShapeDtypeStruct((rows, columns), jnp.bfloat16)] * RING,
        compiler_params=pltpu.CompilerParams(vmem_limit_bytes=16 * 2**20),
    )(*partials, *weights)


def project_kernel(piece_hbm, weight_hbm, out_ref, piece_ref, weight_ref, piece_sem, sem):
    depth = weight_ref.shape[0] // sem.shape[0]
    per_piece = piece_ref.shape[2] // depth

    def fetch(c):
        at = pl.ds(c * depth, depth)
        return pltpu.make_async_copy(weight_hbm.at[at], weight_ref.at[at], sem.at[c])

    pieces = pltpu.make_async_copy(piece_hbm, piece_ref, piece_sem)
    pieces.start()
    for c in range(sem.shape[0]):
        fetch(c).start()
    pieces.wait()
    for c in range(sem.shape[0]):
        fetch(c).wait()
        piece, part = c // per_piece, c % per_piece
        product = jnp.dot(
            piece_ref[piece, :, part * depth : (part + 1) * depth],
            weight_ref[c * depth : (c + 1) * depth, :],
            preferred_element_type=jnp.float32,
        )
        if c == 0:
            out_ref[...] = product
        else:
            out_ref[...] += product


def project(pieces, weights):
    count, requests, features = pieces.shape
    columns = weights.shape[1]
    hbm = pl.BlockSpec(memory_space=pltpu.HBM)
    return pl.pallas_call(
        project_kernel,
        in_specs=[hbm, hbm],
        out_specs=pl.BlockSpec(memory_space=pltpu.VMEM),
        out_shape=jax.ShapeDtypeStruct((requests, columns), jnp.float32),
        scratch_shapes=[
            pltpu.VMEM(pieces.shape, jnp.bfloat16),
            pltpu.VMEM(weights.shape, jnp.bfloat16),
            pltpu.SemaphoreType.DMA,
            pltpu.SemaphoreType.DMA((weights.shape[0] // DEPTH,)),
        ],
        compiler_params=pltpu.CompilerParams(vmem_limit_bytes=52 * 2**20),
        cost_estimate=pl.CostEstimate(
            flops=2 * count * requests * features * columns,
            bytes_accessed=2 * count * features * columns,
            transcendentals=0,
        ),
    )(pieces, weights)


def swap_tensor(value, k):
    return lax.ppermute(value, "tensor", [(i, i ^ k) for i in range(RING)])


def swap_dp(value, k):
    return lax.ppermute(value, "dp", [(i, i ^ k) for i in range(RING * Z_CHIPS * CORES)])


def swap_y(value, k):
    return swap_dp(value, k * Z_CHIPS * CORES)


def swap_z(value, k):
    return swap_dp(value, k * CORES)


def swap_core(value):
    return swap_dp(value, 1)


def on_device(
    queries,
    token_keys,
    token_values,
    cached_key_rows,
    cached_value_rows,
    cache_length,
    output_projection,
    request_adapter,
    adapter_table_row,
    adapter_down_weight,
    adapter_up_weight,
):
    bf16, f32 = jnp.bfloat16, jnp.float32
    requests = queries.shape[0]
    columns = output_projection.shape[1]
    owned = Z_CHIPS * CORES
    here = lax.axis_index("dp")

    down_here, up_here = adapter_down_weight[0], adapter_up_weight[0]
    both = jnp.concatenate([down_here, up_here], axis=1)
    over_z = [swap_z(both, k) for k in range(1, Z_CHIPS)]
    both_other = swap_core(both)

    attended, *placed = attend(
        queries,
        token_keys,
        token_values,
        cached_key_rows,
        cached_value_rows,
        cache_length,
        request_adapter,
        adapter_table_row,
        owned * CAP,
    )
    pieces = lax.all_to_all(attended, "tensor", 0, 0)
    placed, over_z, both_other, request_adapter = lax.optimization_barrier(
        (placed, over_z, both_other, request_adapter)
    )
    routed = [placed[0]] + [swap_y(placed[m], m) for m in range(1, RING)]
    table = [both, both_other]
    for w in over_z:
        table += [w, swap_core(w)]

    every_adapter = adapter_table_row.shape[0]
    matches = request_adapter[:, None] == jnp.arange(every_adapter, dtype=jnp.int32)[None, :]
    slot_of = jnp.sum(jnp.where(matches, adapter_table_row[None, :], 0), axis=1)
    order = jnp.arange(requests, dtype=jnp.int32)
    earlier = (slot_of[:, None] == slot_of[None, :]) & (order[:, None] > order[None, :])
    position = (slot_of ^ here) * CAP + jnp.sum(earlier.astype(jnp.int32), axis=1)
    placing = (
        position[:, None] == jnp.arange(every_adapter * CAP, dtype=jnp.int32)[None, :]
    ).astype(bf16)

    partial = down(routed, table)
    partials = [partial] + [swap_tensor(partial, k) for k in range(1, RING)]
    partials, pieces = lax.optimization_barrier((partials, pieces))
    projected = project(pieces, output_projection)

    delta = up(partials, table, columns)
    back = [delta[0]] + [swap_y(delta[m], m) for m in range(1, RING)]
    returned = jnp.dot(placing, jnp.concatenate(back, axis=0), preferred_element_type=f32)
    return (projected + returned).astype(bf16)


def solution(mesh):
    in_specs = (
        P("dp", "tensor"),
        P("dp", "tensor"),
        P("dp", "tensor"),
        P("dp", None, "tensor"),
        P("dp", None, "tensor"),
        P("dp"),
        P(None, "tensor"),
        P("dp"),
        P(),
        P("dp", None, "tensor"),
        P("dp", None, "tensor"),
    )
    out_specs = P("dp", "tensor")
    return jax.shard_map(
        on_device, mesh=mesh, in_specs=in_specs, out_specs=out_specs, check_vma=False
    )
```

```python
import functools
import math

import jax
import jax.numpy as jnp
from jax import lax
from jax.experimental import pallas as pl
from jax.experimental.pallas import tpu as pltpu
from jax.sharding import PartitionSpec as P

HEADS = 32
KV_HEADS = 4
HEAD_DIM = 128
CAP = 8
Z_CHIPS = 4
CORES = 2
RING = 4
GROUP = HEADS // KV_HEADS
BLOCK = 32
ATTEND_VMEM = 63 * 2**20
STAGED = 6
AHEAD = 2
PROJECT_AHEAD = 3
DEPTH = 512


def slot_positions(request_adapter, table_ref):
    i32, f32 = jnp.int32, jnp.float32
    requests = request_adapter.shape[1]
    slot = jnp.zeros_like(request_adapter)
    for adapter in range(table_ref.shape[0]):
        slot = jnp.where(request_adapter == adapter, table_ref[adapter], slot)
    square = (requests, requests)
    across = jnp.broadcast_to(slot.astype(f32), square)
    earlier = (across.T == across) & (
        lax.broadcasted_iota(i32, square, 0) < lax.broadcasted_iota(i32, square, 1)
    )
    count = jnp.sum(jnp.where(earlier, 1.0, 0.0), axis=0, keepdims=True).astype(i32)
    return (slot ^ lax.axis_index("dp")) * CAP + count


def attend_kernel(*refs):
    sources, (key_hbm, value_hbm), refs = refs[:STAGED], refs[STAGED : STAGED + 2], refs[STAGED + 2 :]
    attended_ref, bucket_refs, refs = refs[0], refs[1 : 1 + RING], refs[1 + RING :]
    staged, refs = refs[:STAGED], refs[STAGED:]
    length_ref, table_ref, adapter_ref, query_ref, token_key_ref, token_value_ref = staged
    key_ref, value_ref, heads_ref, mixed_ref, staged_sem, key_sem, value_sem = refs
    f32, bf16 = jnp.float32, jnp.bfloat16
    requests, positions, _ = key_ref.shape
    blocks = requests // BLOCK
    score_scale = 1.0 / math.sqrt(HEAD_DIM)

    def fetch(source, target, sem, c):
        at = pl.ds(c * BLOCK, BLOCK)
        return pltpu.make_async_copy(source.at[at], target.at[at], sem.at[c])

    staging = [
        pltpu.make_async_copy(source, target, staged_sem.at[i])
        for i, (source, target) in enumerate(zip(sources, staged))
    ]
    for copy in staging:
        copy.start()
    def start(c):
        fetch(key_hbm, key_ref, key_sem, c).start()
        fetch(value_hbm, value_ref, value_sem, c).start()

    for c in range(min(AHEAD, blocks)):
        start(c)
    for copy in staging:
        copy.wait()
    slots_at = slot_positions(adapter_ref[...], table_ref)

    for c in range(blocks):
        if c + AHEAD < blocks:
            start(c + AHEAD)
        rows = slice(c * BLOCK, (c + 1) * BLOCK)
        for h in range(GROUP):
            heads_ref[pl.ds(h, BLOCK, stride=GROUP), :] = query_ref[
                rows, h * HEAD_DIM : (h + 1) * HEAD_DIM
            ].astype(f32)
        heads = heads_ref[...].reshape(BLOCK, GROUP, HEAD_DIM)
        fresh_keys = token_key_ref[rows, :].astype(f32)[:, None, :]
        fresh_values = token_value_ref[rows, :].astype(f32)[:, None, :]
        fetch(key_hbm, key_ref, key_sem, c).wait()
        score = score_scale * lax.dot_general(
            heads.astype(bf16),
            key_ref[rows],
            (((2,), (2,)), ((0,), (0,))),
            preferred_element_type=f32,
        )
        fresh = jnp.sum(heads * fresh_keys, axis=2, keepdims=True) * score_scale
        place = lax.broadcasted_iota(jnp.int32, (GROUP, positions), 1)
        score = jnp.stack(
            [
                jnp.where(place < length_ref[c * BLOCK + r], score[r], -jnp.inf)
                for r in range(BLOCK)
            ]
        )
        row_max = jnp.maximum(jnp.max(score, axis=2, keepdims=True), fresh)
        weight = jnp.exp(score - row_max)
        fresh_weight = jnp.exp(fresh - row_max)
        weight_sum = jnp.sum(weight, axis=2, keepdims=True) + fresh_weight
        fetch(value_hbm, value_ref, value_sem, c).wait()
        mixed = lax.dot_general(
            weight.astype(bf16),
            value_ref[rows],
            (((2,), (1,)), ((0,), (0,))),
            preferred_element_type=f32,
        )
        mixed = mixed + fresh_weight.astype(bf16).astype(f32) * fresh_values
        mixed_ref[...] = (mixed / weight_sum).reshape(BLOCK * GROUP, HEAD_DIM)
        for h in range(GROUP):
            attended_ref[0, rows, h * HEAD_DIM : (h + 1) * HEAD_DIM] = mixed_ref[
                pl.ds(h, BLOCK, stride=GROUP), :
            ].astype(bf16)

    attended = attended_ref[0]
    for k in range(1, RING):
        attended_ref[k] = attended
    for m, bucket_ref in enumerate(bucket_refs):
        slots = bucket_ref.shape[0]
        wanted = m * slots + lax.broadcasted_iota(jnp.int32, (slots, requests), 0)
        placing = jnp.where(wanted == slots_at, 1.0, 0.0).astype(bf16)
        bucket_ref[...] = jnp.dot(placing, attended, preferred_element_type=f32).astype(bf16)


def attend(
    queries,
    token_keys,
    token_values,
    cached_key_rows,
    cached_value_rows,
    cache_length,
    request_adapter,
    adapter_table_row,
    slots,
):
    requests, features = queries.shape
    positions = cached_key_rows.shape[1]
    vmem = pl.BlockSpec(memory_space=pltpu.VMEM)
    hbm = pl.BlockSpec(memory_space=pltpu.HBM)
    per_head = pltpu.VMEM((BLOCK * GROUP, HEAD_DIM), jnp.float32)
    fetches = pltpu.SemaphoreType.DMA((requests // BLOCK,))
    return pl.pallas_call(
        attend_kernel,
        in_specs=[hbm] * (STAGED + 2),
        out_specs=[vmem] * (1 + RING),
        out_shape=[jax.ShapeDtypeStruct((RING, requests, features), jnp.bfloat16)]
        + [jax.ShapeDtypeStruct((slots, features), jnp.bfloat16)] * RING,
        scratch_shapes=[
            pltpu.SMEM(cache_length.shape, jnp.int32),
            pltpu.SMEM(adapter_table_row.shape, jnp.int32),
            pltpu.VMEM((1, requests), jnp.int32),
            pltpu.VMEM(queries.shape, jnp.bfloat16),
            pltpu.VMEM(token_keys.shape, jnp.bfloat16),
            pltpu.VMEM(token_values.shape, jnp.bfloat16),
        ]
        + [pltpu.VMEM(cached_key_rows.shape, jnp.bfloat16)] * 2
        + [per_head] * 2
        + [pltpu.SemaphoreType.DMA((STAGED,)), fetches, fetches],
        compiler_params=pltpu.CompilerParams(vmem_limit_bytes=ATTEND_VMEM),
        cost_estimate=pl.CostEstimate(
            flops=4 * requests * GROUP * positions * HEAD_DIM,
            bytes_accessed=4 * requests * positions * HEAD_DIM,
            transcendentals=requests * GROUP * positions,
        ),
    )(
        cache_length,
        adapter_table_row,
        request_adapter.reshape(1, requests),
        queries,
        token_keys,
        token_values,
        cached_key_rows,
        cached_value_rows,
    )


def down_kernel(*refs):
    routed, weights, out_ref = refs[:RING], refs[RING:-1], refs[-1]
    rank = weights[0].shape[0]
    features = routed[0].shape[1]
    pair = CORES * CAP
    for k in range(Z_CHIPS):
        rows = jnp.concatenate([r[k * pair : (k + 1) * pair, :] for r in routed], axis=0)
        products = [
            lax.dot_general(
                rows,
                w[:, :features],
                (((1,), (1,)), ((), ())),
                preferred_element_type=jnp.float32,
            )
            for w in weights[k * CORES : (k + 1) * CORES]
        ]
        for m in range(RING):
            at = (k * RING + m) * CAP
            for j, product in enumerate(products):
                row = m * pair + j * CAP
                out_ref[at : at + CAP, j * rank : (j + 1) * rank] = product[row : row + CAP, :]


def down(routed, weights):
    rank = weights[0].shape[0]
    vmem = pl.BlockSpec(memory_space=pltpu.VMEM)
    return pl.pallas_call(
        down_kernel,
        in_specs=[vmem] * (len(routed) + len(weights)),
        out_specs=vmem,
        out_shape=jax.ShapeDtypeStruct((Z_CHIPS * RING * CAP, CORES * rank), jnp.float32),
        compiler_params=pltpu.CompilerParams(vmem_limit_bytes=16 * 2**20),
    )(*routed, *weights)


def up_kernel(columns, *refs):
    partials, weights, deltas = refs[:RING], refs[RING:-RING], refs[-RING:]
    rank = weights[0].shape[0]
    pair = CORES * CAP
    total = partials[0][...] + partials[1][...] + partials[2][...] + partials[3][...]
    for k in range(Z_CHIPS):
        part = total[k * RING * CAP : (k + 1) * RING * CAP, :]
        spread = []
        for m in range(RING):
            spread += [part[m * CAP : (m + 1) * CAP, :]] * CORES
        spread = jnp.concatenate(spread, axis=0)
        row = lax.broadcasted_iota(jnp.int32, spread.shape, 0)
        lane = lax.broadcasted_iota(jnp.int32, spread.shape, 1)
        low_rank = jnp.where((row // CAP) % CORES == lane // rank, spread, 0.0)
        low_rank = low_rank.astype(jnp.bfloat16)
        delta = 0.0
        for j, w in enumerate(weights[k * CORES : (k + 1) * CORES]):
            delta += jnp.dot(
                low_rank[:, j * rank : (j + 1) * rank],
                w[:, w.shape[1] - columns :],
                preferred_element_type=jnp.float32,
            )
        delta = delta.astype(jnp.bfloat16)
        for m, delta_ref in enumerate(deltas):
            delta_ref[k * pair : (k + 1) * pair, :] = delta[m * pair : (m + 1) * pair, :]


def up(partials, weights, columns):
    rows = Z_CHIPS * CORES * CAP
    vmem = pl.BlockSpec(memory_space=pltpu.VMEM)
    return pl.pallas_call(
        functools.partial(up_kernel, columns),
        in_specs=[vmem] * (len(partials) + len(weights)),
        out_specs=[vmem] * RING,
        out_shape=[jax.ShapeDtypeStruct((rows, columns), jnp.bfloat16)] * RING,
        compiler_params=pltpu.CompilerParams(vmem_limit_bytes=16 * 2**20),
    )(*partials, *weights)


def project_kernel(piece_hbm, weight_hbm, out_ref, piece_ref, weight_ref, piece_sem, sem):
    depth = weight_ref.shape[0] // sem.shape[0]
    per_piece = piece_ref.shape[2] // depth

    def fetch(c):
        at = pl.ds(c * depth, depth)
        return pltpu.make_async_copy(weight_hbm.at[at], weight_ref.at[at], sem.at[c])

    pieces = pltpu.make_async_copy(piece_hbm, piece_ref, piece_sem)
    pieces.start()
    count = sem.shape[0]
    for c in range(min(PROJECT_AHEAD, count)):
        fetch(c).start()
    pieces.wait()
    for c in range(count):
        if c + PROJECT_AHEAD < count:
            fetch(c + PROJECT_AHEAD).start()
        fetch(c).wait()
        piece, part = c // per_piece, c % per_piece
        product = jnp.dot(
            piece_ref[piece, :, part * depth : (part + 1) * depth],
            weight_ref[c * depth : (c + 1) * depth, :],
            preferred_element_type=jnp.float32,
        )
        if c == 0:
            out_ref[...] = product
        else:
            out_ref[...] += product


def project(pieces, weights):
    count, requests, features = pieces.shape
    columns = weights.shape[1]
    hbm = pl.BlockSpec(memory_space=pltpu.HBM)
    return pl.pallas_call(
        project_kernel,
        in_specs=[hbm, hbm],
        out_specs=pl.BlockSpec(memory_space=pltpu.VMEM),
        out_shape=jax.ShapeDtypeStruct((requests, columns), jnp.float32),
        scratch_shapes=[
            pltpu.VMEM(pieces.shape, jnp.bfloat16),
            pltpu.VMEM(weights.shape, jnp.bfloat16),
            pltpu.SemaphoreType.DMA,
            pltpu.SemaphoreType.DMA((weights.shape[0] // DEPTH,)),
        ],
        compiler_params=pltpu.CompilerParams(vmem_limit_bytes=52 * 2**20),
        cost_estimate=pl.CostEstimate(
            flops=2 * count * requests * features * columns,
            bytes_accessed=2 * count * features * columns,
            transcendentals=0,
        ),
    )(pieces, weights)


def swap_tensor(value, k):
    return lax.ppermute(value, "tensor", [(i, i ^ k) for i in range(RING)])


def swap_dp(value, k):
    return lax.ppermute(value, "dp", [(i, i ^ k) for i in range(RING * Z_CHIPS * CORES)])


def swap_y(value, k):
    return swap_dp(value, k * Z_CHIPS * CORES)


def swap_z(value, k):
    return swap_dp(value, k * CORES)


def swap_core(value):
    return swap_dp(value, 1)


def on_device(
    queries,
    token_keys,
    token_values,
    cached_key_rows,
    cached_value_rows,
    cache_length,
    output_projection,
    request_adapter,
    adapter_table_row,
    adapter_down_weight,
    adapter_up_weight,
):
    bf16, f32 = jnp.bfloat16, jnp.float32
    requests = queries.shape[0]
    columns = output_projection.shape[1]
    owned = Z_CHIPS * CORES
    here = lax.axis_index("dp")

    down_here, up_here = adapter_down_weight[0], adapter_up_weight[0]
    both = jnp.concatenate([down_here, up_here], axis=1)
    beside = [swap_z(both, k) for k in (1, 3)]
    both_other = swap_core(both)

    attended, *placed = attend(
        queries,
        token_keys,
        token_values,
        cached_key_rows,
        cached_value_rows,
        cache_length,
        request_adapter,
        adapter_table_row,
        owned * CAP,
    )
    pieces = lax.all_to_all(attended, "tensor", 0, 0)
    placed, beside, both_late, request_adapter = lax.optimization_barrier(
        (placed, beside, both, request_adapter)
    )
    across = swap_z(both_late, 2)
    beside_other = [swap_core(w) for w in beside]
    placed, beside_other, both_other = lax.optimization_barrier(
        (placed, beside_other, both_other)
    )
    routed = [placed[0]] + [swap_y(placed[m], m) for m in range(1, RING)]
    routed, across = lax.optimization_barrier((routed, across))
    table = [both, both_other, beside[0], beside_other[0]]
    table += [across, swap_core(across), beside[1], beside_other[1]]

    every_adapter = adapter_table_row.shape[0]
    matches = request_adapter[:, None] == jnp.arange(every_adapter, dtype=jnp.int32)[None, :]
    slot_of = jnp.sum(jnp.where(matches, adapter_table_row[None, :], 0), axis=1)
    order = jnp.arange(requests, dtype=jnp.int32)
    earlier = (slot_of[:, None] == slot_of[None, :]) & (order[:, None] > order[None, :])
    position = (slot_of ^ here) * CAP + jnp.sum(earlier.astype(jnp.int32), axis=1)
    placing = (
        position[:, None] == jnp.arange(every_adapter * CAP, dtype=jnp.int32)[None, :]
    ).astype(bf16)

    partial = down(routed, table)
    partials = [partial] + [swap_tensor(partial, k) for k in range(1, RING)]
    partials, pieces = lax.optimization_barrier((partials, pieces))
    projected = project(pieces, output_projection)

    delta = up(partials, table, columns)
    back = [delta[0]] + [swap_y(delta[m], m) for m in range(1, RING)]
    returned = jnp.dot(placing, jnp.concatenate(back, axis=0), preferred_element_type=f32)
    return (projected + returned).astype(bf16)


def solution(mesh):
    in_specs = (
        P("dp", "tensor"),
        P("dp", "tensor"),
        P("dp", "tensor"),
        P("dp", None, "tensor"),
        P("dp", None, "tensor"),
        P("dp"),
        P(None, "tensor"),
        P("dp"),
        P(),
        P("dp", None, "tensor"),
        P("dp", None, "tensor"),
    )
    out_specs = P("dp", "tensor")
    return jax.shard_map(
        on_device, mesh=mesh, in_specs=in_specs, out_specs=out_specs, check_vma=False
    )
```

```python
import functools
import math

import jax
import jax.numpy as jnp
from jax import lax
from jax.experimental import pallas as pl
from jax.experimental.pallas import tpu as pltpu
from jax.sharding import PartitionSpec as P

HEADS = 32
KV_HEADS = 4
HEAD_DIM = 128
CAP = 8
Z_CHIPS = 4
CORES = 2
RING = 4
GROUP = HEADS // KV_HEADS
BLOCK = 32
ATTEND_VMEM = 63 * 2**20
STAGED = 6
AHEAD = 2
PROJECT_AHEAD = 3
DEPTH = 512


def slot_positions(request_adapter, table_ref):
    i32, f32 = jnp.int32, jnp.float32
    requests = request_adapter.shape[1]
    slot = jnp.zeros_like(request_adapter)
    for adapter in range(table_ref.shape[0]):
        slot = jnp.where(request_adapter == adapter, table_ref[adapter], slot)
    square = (requests, requests)
    across = jnp.broadcast_to(slot.astype(f32), square)
    earlier = (across.T == across) & (
        lax.broadcasted_iota(i32, square, 0) < lax.broadcasted_iota(i32, square, 1)
    )
    count = jnp.sum(jnp.where(earlier, 1.0, 0.0), axis=0, keepdims=True).astype(i32)
    return (slot ^ lax.axis_index("dp")) * CAP + count


def attend_kernel(*refs):
    sources, (key_hbm, value_hbm), refs = refs[:STAGED], refs[STAGED : STAGED + 2], refs[STAGED + 2 :]
    attended_ref, bucket_refs, refs = refs[0], refs[1 : 1 + RING], refs[1 + RING :]
    staged, refs = refs[:STAGED], refs[STAGED:]
    length_ref, table_ref, adapter_ref, query_ref, token_key_ref, token_value_ref = staged
    key_ref, value_ref, heads_ref, mixed_ref, staged_sem, key_sem, value_sem = refs
    f32, bf16 = jnp.float32, jnp.bfloat16
    requests, positions, _ = key_ref.shape
    blocks = requests // BLOCK
    score_scale = 1.0 / math.sqrt(HEAD_DIM)

    def fetch(source, target, sem, c):
        at = pl.ds(c * BLOCK, BLOCK)
        return pltpu.make_async_copy(source.at[at], target.at[at], sem.at[c])

    staging = [
        pltpu.make_async_copy(source, target, staged_sem.at[i])
        for i, (source, target) in enumerate(zip(sources, staged))
    ]
    for copy in staging:
        copy.start()
    def start(c):
        fetch(key_hbm, key_ref, key_sem, c).start()
        fetch(value_hbm, value_ref, value_sem, c).start()

    for c in range(min(AHEAD, blocks)):
        start(c)
    for copy in staging:
        copy.wait()
    slots_at = slot_positions(adapter_ref[...], table_ref)

    for c in range(blocks):
        if c + AHEAD < blocks:
            start(c + AHEAD)
        rows = slice(c * BLOCK, (c + 1) * BLOCK)
        for h in range(GROUP):
            heads_ref[pl.ds(h, BLOCK, stride=GROUP), :] = query_ref[
                rows, h * HEAD_DIM : (h + 1) * HEAD_DIM
            ].astype(f32)
        heads = heads_ref[...].reshape(BLOCK, GROUP, HEAD_DIM)
        fresh_keys = token_key_ref[rows, :].astype(f32)[:, None, :]
        fresh_values = token_value_ref[rows, :].astype(f32)[:, None, :]
        fetch(key_hbm, key_ref, key_sem, c).wait()
        score = score_scale * lax.dot_general(
            heads.astype(bf16),
            key_ref[rows],
            (((2,), (2,)), ((0,), (0,))),
            preferred_element_type=f32,
        )
        fresh = jnp.sum(heads * fresh_keys, axis=2, keepdims=True) * score_scale
        place = lax.broadcasted_iota(jnp.int32, (GROUP, positions), 1)
        score = jnp.stack(
            [
                jnp.where(place < length_ref[c * BLOCK + r], score[r], -jnp.inf)
                for r in range(BLOCK)
            ]
        )
        row_max = jnp.maximum(jnp.max(score, axis=2, keepdims=True), fresh)
        weight = jnp.exp(score - row_max)
        fresh_weight = jnp.exp(fresh - row_max)
        weight_sum = jnp.sum(weight, axis=2, keepdims=True) + fresh_weight
        fetch(value_hbm, value_ref, value_sem, c).wait()
        mixed = lax.dot_general(
            weight.astype(bf16),
            value_ref[rows],
            (((2,), (1,)), ((0,), (0,))),
            preferred_element_type=f32,
        )
        mixed = mixed + fresh_weight.astype(bf16).astype(f32) * fresh_values
        mixed_ref[...] = (mixed / weight_sum).reshape(BLOCK * GROUP, HEAD_DIM)
        for h in range(GROUP):
            attended_ref[0, rows, h * HEAD_DIM : (h + 1) * HEAD_DIM] = mixed_ref[
                pl.ds(h, BLOCK, stride=GROUP), :
            ].astype(bf16)

    attended = attended_ref[0]
    for k in range(1, RING):
        attended_ref[k] = attended
    for m, bucket_ref in enumerate(bucket_refs):
        slots = bucket_ref.shape[0]
        wanted = m * slots + lax.broadcasted_iota(jnp.int32, (slots, requests), 0)
        placing = jnp.where(wanted == slots_at, 1.0, 0.0).astype(bf16)
        bucket_ref[...] = jnp.dot(placing, attended, preferred_element_type=f32).astype(bf16)


def attend(
    queries,
    token_keys,
    token_values,
    cached_key_rows,
    cached_value_rows,
    cache_length,
    request_adapter,
    adapter_table_row,
    slots,
):
    requests, features = queries.shape
    positions = cached_key_rows.shape[1]
    vmem = pl.BlockSpec(memory_space=pltpu.VMEM)
    hbm = pl.BlockSpec(memory_space=pltpu.HBM)
    per_head = pltpu.VMEM((BLOCK * GROUP, HEAD_DIM), jnp.float32)
    fetches = pltpu.SemaphoreType.DMA((requests // BLOCK,))
    return pl.pallas_call(
        attend_kernel,
        in_specs=[hbm] * (STAGED + 2),
        out_specs=[vmem] * (1 + RING),
        out_shape=[jax.ShapeDtypeStruct((RING, requests, features), jnp.bfloat16)]
        + [jax.ShapeDtypeStruct((slots, features), jnp.bfloat16)] * RING,
        scratch_shapes=[
            pltpu.SMEM(cache_length.shape, jnp.int32),
            pltpu.SMEM(adapter_table_row.shape, jnp.int32),
            pltpu.VMEM((1, requests), jnp.int32),
            pltpu.VMEM(queries.shape, jnp.bfloat16),
            pltpu.VMEM(token_keys.shape, jnp.bfloat16),
            pltpu.VMEM(token_values.shape, jnp.bfloat16),
        ]
        + [pltpu.VMEM(cached_key_rows.shape, jnp.bfloat16)] * 2
        + [per_head] * 2
        + [pltpu.SemaphoreType.DMA((STAGED,)), fetches, fetches],
        compiler_params=pltpu.CompilerParams(vmem_limit_bytes=ATTEND_VMEM),
        cost_estimate=pl.CostEstimate(
            flops=4 * requests * GROUP * positions * HEAD_DIM,
            bytes_accessed=4 * requests * positions * HEAD_DIM,
            transcendentals=requests * GROUP * positions,
        ),
    )(
        cache_length,
        adapter_table_row,
        request_adapter.reshape(1, requests),
        queries,
        token_keys,
        token_values,
        cached_key_rows,
        cached_value_rows,
    )


def down_kernel(*refs):
    routed, weights, out_ref = refs[:RING], refs[RING:-1], refs[-1]
    rank = weights[0].shape[0]
    features = routed[0].shape[1]
    pair = CORES * CAP
    for k in range(Z_CHIPS):
        rows = jnp.concatenate([r[k * pair : (k + 1) * pair, :] for r in routed], axis=0)
        products = [
            lax.dot_general(
                rows,
                w[:, :features],
                (((1,), (1,)), ((), ())),
                preferred_element_type=jnp.float32,
            )
            for w in weights[k * CORES : (k + 1) * CORES]
        ]
        for m in range(RING):
            at = (k * RING + m) * CAP
            for j, product in enumerate(products):
                row = m * pair + j * CAP
                out_ref[at : at + CAP, j * rank : (j + 1) * rank] = product[row : row + CAP, :]


def down(routed, weights):
    rank = weights[0].shape[0]
    vmem = pl.BlockSpec(memory_space=pltpu.VMEM)
    return pl.pallas_call(
        down_kernel,
        in_specs=[vmem] * (len(routed) + len(weights)),
        out_specs=vmem,
        out_shape=jax.ShapeDtypeStruct((Z_CHIPS * RING * CAP, CORES * rank), jnp.float32),
        compiler_params=pltpu.CompilerParams(vmem_limit_bytes=16 * 2**20),
    )(*routed, *weights)


def up_kernel(columns, *refs):
    partials, weights, deltas = refs[:RING], refs[RING:-RING], refs[-RING:]
    rank = weights[0].shape[0]
    pair = CORES * CAP
    total = partials[0][...] + partials[1][...] + partials[2][...] + partials[3][...]
    for k in range(Z_CHIPS):
        part = total[k * RING * CAP : (k + 1) * RING * CAP, :]
        spread = []
        for m in range(RING):
            spread += [part[m * CAP : (m + 1) * CAP, :]] * CORES
        spread = jnp.concatenate(spread, axis=0)
        row = lax.broadcasted_iota(jnp.int32, spread.shape, 0)
        lane = lax.broadcasted_iota(jnp.int32, spread.shape, 1)
        low_rank = jnp.where((row // CAP) % CORES == lane // rank, spread, 0.0)
        low_rank = low_rank.astype(jnp.bfloat16)
        delta = 0.0
        for j, w in enumerate(weights[k * CORES : (k + 1) * CORES]):
            delta += jnp.dot(
                low_rank[:, j * rank : (j + 1) * rank],
                w[:, w.shape[1] - columns :],
                preferred_element_type=jnp.float32,
            )
        delta = delta.astype(jnp.bfloat16)
        for m, delta_ref in enumerate(deltas):
            delta_ref[k * pair : (k + 1) * pair, :] = delta[m * pair : (m + 1) * pair, :]


def up(partials, weights, columns):
    rows = Z_CHIPS * CORES * CAP
    vmem = pl.BlockSpec(memory_space=pltpu.VMEM)
    return pl.pallas_call(
        functools.partial(up_kernel, columns),
        in_specs=[vmem] * (len(partials) + len(weights)),
        out_specs=[vmem] * RING,
        out_shape=[jax.ShapeDtypeStruct((rows, columns), jnp.bfloat16)] * RING,
        compiler_params=pltpu.CompilerParams(vmem_limit_bytes=16 * 2**20),
    )(*partials, *weights)


def project_kernel(piece_hbm, weight_hbm, out_ref, piece_ref, weight_ref, piece_sem, sem):
    depth = weight_ref.shape[0] // sem.shape[0]
    per_piece = piece_ref.shape[2] // depth

    def fetch(c):
        at = pl.ds(c * depth, depth)
        return pltpu.make_async_copy(weight_hbm.at[at], weight_ref.at[at], sem.at[c])

    pieces = pltpu.make_async_copy(piece_hbm, piece_ref, piece_sem)
    pieces.start()
    count = sem.shape[0]
    for c in range(min(PROJECT_AHEAD, count)):
        fetch(c).start()
    pieces.wait()
    for c in range(count):
        if c + PROJECT_AHEAD < count:
            fetch(c + PROJECT_AHEAD).start()
        fetch(c).wait()
        piece, part = c // per_piece, c % per_piece
        product = jnp.dot(
            piece_ref[piece, :, part * depth : (part + 1) * depth],
            weight_ref[c * depth : (c + 1) * depth, :],
            preferred_element_type=jnp.float32,
        )
        if c == 0:
            out_ref[...] = product
        else:
            out_ref[...] += product


def project(pieces, weights):
    count, requests, features = pieces.shape
    columns = weights.shape[1]
    hbm = pl.BlockSpec(memory_space=pltpu.HBM)
    return pl.pallas_call(
        project_kernel,
        in_specs=[hbm, hbm],
        out_specs=pl.BlockSpec(memory_space=pltpu.VMEM),
        out_shape=jax.ShapeDtypeStruct((requests, columns), jnp.float32),
        scratch_shapes=[
            pltpu.VMEM(pieces.shape, jnp.bfloat16),
            pltpu.VMEM(weights.shape, jnp.bfloat16),
            pltpu.SemaphoreType.DMA,
            pltpu.SemaphoreType.DMA((weights.shape[0] // DEPTH,)),
        ],
        compiler_params=pltpu.CompilerParams(vmem_limit_bytes=52 * 2**20),
        cost_estimate=pl.CostEstimate(
            flops=2 * count * requests * features * columns,
            bytes_accessed=2 * count * features * columns,
            transcendentals=0,
        ),
    )(pieces, weights)


def swap_tensor(value, k):
    return lax.ppermute(value, "tensor", [(i, i ^ k) for i in range(RING)])


def swap_dp(value, k):
    return lax.ppermute(value, "dp", [(i, i ^ k) for i in range(RING * Z_CHIPS * CORES)])


def swap_y(value, k):
    return swap_dp(value, k * Z_CHIPS * CORES)


def swap_z(value, k):
    return swap_dp(value, k * CORES)


def swap_core(value):
    return swap_dp(value, 1)


def on_device(
    queries,
    token_keys,
    token_values,
    cached_key_rows,
    cached_value_rows,
    cache_length,
    output_projection,
    request_adapter,
    adapter_table_row,
    adapter_down_weight,
    adapter_up_weight,
):
    bf16, f32 = jnp.bfloat16, jnp.float32
    requests = queries.shape[0]
    columns = output_projection.shape[1]
    owned = Z_CHIPS * CORES
    here = lax.axis_index("dp")

    down_here, up_here = adapter_down_weight[0], adapter_up_weight[0]
    both = jnp.concatenate([down_here, up_here], axis=1)
    beside = [swap_z(both, k) for k in (1, 3)]
    both_other = swap_core(both)

    attended, *placed = attend(
        queries,
        token_keys,
        token_values,
        cached_key_rows,
        cached_value_rows,
        cache_length,
        request_adapter,
        adapter_table_row,
        owned * CAP,
    )
    pieces = lax.all_to_all(attended, "tensor", 0, 0)
    placed, both_late, request_adapter = lax.optimization_barrier(
        (placed, both, request_adapter)
    )
    across = swap_z(both_late, 2)
    placed, beside, both_other = lax.optimization_barrier((placed, beside, both_other))
    beside_other = [swap_core(w) for w in beside]
    routed = [placed[0]] + [swap_y(placed[m], m) for m in range(1, RING)]
    routed, across = lax.optimization_barrier((routed, across))
    table = [both, both_other, beside[0], beside_other[0]]
    table += [across, swap_core(across), beside[1], beside_other[1]]

    every_adapter = adapter_table_row.shape[0]
    matches = request_adapter[:, None] == jnp.arange(every_adapter, dtype=jnp.int32)[None, :]
    slot_of = jnp.sum(jnp.where(matches, adapter_table_row[None, :], 0), axis=1)
    order = jnp.arange(requests, dtype=jnp.int32)
    earlier = (slot_of[:, None] == slot_of[None, :]) & (order[:, None] > order[None, :])
    position = (slot_of ^ here) * CAP + jnp.sum(earlier.astype(jnp.int32), axis=1)
    placing = (
        position[:, None] == jnp.arange(every_adapter * CAP, dtype=jnp.int32)[None, :]
    ).astype(bf16)

    partial = down(routed, table)
    partials = [partial] + [swap_tensor(partial, k) for k in range(1, RING)]
    partials, pieces = lax.optimization_barrier((partials, pieces))
    projected = project(pieces, output_projection)

    delta = up(partials, table, columns)
    back = [delta[0]] + [swap_y(delta[m], m) for m in range(1, RING)]
    returned = jnp.dot(placing, jnp.concatenate(back, axis=0), preferred_element_type=f32)
    return (projected + returned).astype(bf16)


def solution(mesh):
    in_specs = (
        P("dp", "tensor"),
        P("dp", "tensor"),
        P("dp", "tensor"),
        P("dp", None, "tensor"),
        P("dp", None, "tensor"),
        P("dp"),
        P(None, "tensor"),
        P("dp"),
        P(),
        P("dp", None, "tensor"),
        P("dp", None, "tensor"),
    )
    out_specs = P("dp", "tensor")
    return jax.shard_map(
        on_device, mesh=mesh, in_specs=in_specs, out_specs=out_specs, check_vma=False
    )
```

```python
import functools
import math

import jax
import jax.numpy as jnp
from jax import lax
from jax.experimental import pallas as pl
from jax.experimental.pallas import tpu as pltpu
from jax.sharding import PartitionSpec as P

HEADS = 32
KV_HEADS = 4
HEAD_DIM = 128
CAP = 8
Z_CHIPS = 4
CORES = 2
RING = 4
GROUP = HEADS // KV_HEADS
BLOCKS = (16, 32, 32, 32, 16)
ATTEND_VMEM = 63 * 2**20
STAGED = 6
AHEAD = 2
PROJECT_AHEAD = 3
DEPTH = 512


def slot_positions(request_adapter, table_ref):
    i32, f32 = jnp.int32, jnp.float32
    requests = request_adapter.shape[1]
    slot = jnp.zeros_like(request_adapter)
    for adapter in range(table_ref.shape[0]):
        slot = jnp.where(request_adapter == adapter, table_ref[adapter], slot)
    square = (requests, requests)
    across = jnp.broadcast_to(slot.astype(f32), square)
    earlier = (across.T == across) & (
        lax.broadcasted_iota(i32, square, 0) < lax.broadcasted_iota(i32, square, 1)
    )
    count = jnp.sum(jnp.where(earlier, 1.0, 0.0), axis=0, keepdims=True).astype(i32)
    return (slot ^ lax.axis_index("dp")) * CAP + count


def attend_kernel(*refs):
    sources, (key_hbm, value_hbm), refs = refs[:STAGED], refs[STAGED : STAGED + 2], refs[STAGED + 2 :]
    attended_ref, bucket_refs, refs = refs[0], refs[1 : 1 + RING], refs[1 + RING :]
    staged, refs = refs[:STAGED], refs[STAGED:]
    length_ref, table_ref, adapter_ref, query_ref, token_key_ref, token_value_ref = staged
    key_ref, value_ref, heads_ref, mixed_ref, staged_sem, key_sem, value_sem = refs
    f32, bf16 = jnp.float32, jnp.bfloat16
    requests, positions, _ = key_ref.shape
    blocks = len(BLOCKS)
    score_scale = 1.0 / math.sqrt(HEAD_DIM)

    def fetch(source, target, sem, c):
        at = pl.ds(sum(BLOCKS[:c]), BLOCKS[c])
        return pltpu.make_async_copy(source.at[at], target.at[at], sem.at[c])

    staging = [
        pltpu.make_async_copy(source, target, staged_sem.at[i])
        for i, (source, target) in enumerate(zip(sources, staged))
    ]
    for copy in staging:
        copy.start()
    def start(c):
        fetch(key_hbm, key_ref, key_sem, c).start()
        fetch(value_hbm, value_ref, value_sem, c).start()

    for c in range(min(AHEAD, blocks)):
        start(c)
    for copy in staging:
        copy.wait()
    slots_at = slot_positions(adapter_ref[...], table_ref)

    for c in range(blocks):
        if c + AHEAD < blocks:
            start(c + AHEAD)
        first, block = sum(BLOCKS[:c]), BLOCKS[c]
        rows = slice(first, first + block)
        for h in range(GROUP):
            heads_ref[pl.ds(h, block, stride=GROUP), :] = query_ref[
                rows, h * HEAD_DIM : (h + 1) * HEAD_DIM
            ].astype(f32)
        heads = heads_ref[: block * GROUP, :].reshape(block, GROUP, HEAD_DIM)
        fresh_keys = token_key_ref[rows, :].astype(f32)[:, None, :]
        fresh_values = token_value_ref[rows, :].astype(f32)[:, None, :]
        fetch(key_hbm, key_ref, key_sem, c).wait()
        score = score_scale * lax.dot_general(
            heads.astype(bf16),
            key_ref[rows],
            (((2,), (2,)), ((0,), (0,))),
            preferred_element_type=f32,
        )
        fresh = jnp.sum(heads * fresh_keys, axis=2, keepdims=True) * score_scale
        place = lax.broadcasted_iota(jnp.int32, (GROUP, positions), 1)
        score = jnp.stack(
            [
                jnp.where(place < length_ref[first + r], score[r], -jnp.inf)
                for r in range(block)
            ]
        )
        row_max = jnp.maximum(jnp.max(score, axis=2, keepdims=True), fresh)
        weight = jnp.exp(score - row_max)
        fresh_weight = jnp.exp(fresh - row_max)
        weight_sum = jnp.sum(weight, axis=2, keepdims=True) + fresh_weight
        fetch(value_hbm, value_ref, value_sem, c).wait()
        mixed = lax.dot_general(
            weight.astype(bf16),
            value_ref[rows],
            (((2,), (1,)), ((0,), (0,))),
            preferred_element_type=f32,
        )
        mixed = mixed + fresh_weight.astype(bf16).astype(f32) * fresh_values
        mixed_ref[: block * GROUP, :] = (mixed / weight_sum).reshape(block * GROUP, HEAD_DIM)
        for h in range(GROUP):
            attended_ref[0, rows, h * HEAD_DIM : (h + 1) * HEAD_DIM] = mixed_ref[
                pl.ds(h, block, stride=GROUP), :
            ].astype(bf16)

    attended = attended_ref[0]
    for k in range(1, RING):
        attended_ref[k] = attended
    for m, bucket_ref in enumerate(bucket_refs):
        slots = bucket_ref.shape[0]
        wanted = m * slots + lax.broadcasted_iota(jnp.int32, (slots, requests), 0)
        placing = jnp.where(wanted == slots_at, 1.0, 0.0).astype(bf16)
        bucket_ref[...] = jnp.dot(placing, attended, preferred_element_type=f32).astype(bf16)


def attend(
    queries,
    token_keys,
    token_values,
    cached_key_rows,
    cached_value_rows,
    cache_length,
    request_adapter,
    adapter_table_row,
    slots,
):
    requests, features = queries.shape
    positions = cached_key_rows.shape[1]
    vmem = pl.BlockSpec(memory_space=pltpu.VMEM)
    hbm = pl.BlockSpec(memory_space=pltpu.HBM)
    per_head = pltpu.VMEM((max(BLOCKS) * GROUP, HEAD_DIM), jnp.float32)
    fetches = pltpu.SemaphoreType.DMA((len(BLOCKS),))
    return pl.pallas_call(
        attend_kernel,
        in_specs=[hbm] * (STAGED + 2),
        out_specs=[vmem] * (1 + RING),
        out_shape=[jax.ShapeDtypeStruct((RING, requests, features), jnp.bfloat16)]
        + [jax.ShapeDtypeStruct((slots, features), jnp.bfloat16)] * RING,
        scratch_shapes=[
            pltpu.SMEM(cache_length.shape, jnp.int32),
            pltpu.SMEM(adapter_table_row.shape, jnp.int32),
            pltpu.VMEM((1, requests), jnp.int32),
            pltpu.VMEM(queries.shape, jnp.bfloat16),
            pltpu.VMEM(token_keys.shape, jnp.bfloat16),
            pltpu.VMEM(token_values.shape, jnp.bfloat16),
        ]
        + [pltpu.VMEM(cached_key_rows.shape, jnp.bfloat16)] * 2
        + [per_head] * 2
        + [pltpu.SemaphoreType.DMA((STAGED,)), fetches, fetches],
        compiler_params=pltpu.CompilerParams(vmem_limit_bytes=ATTEND_VMEM),
        cost_estimate=pl.CostEstimate(
            flops=4 * requests * GROUP * positions * HEAD_DIM,
            bytes_accessed=4 * requests * positions * HEAD_DIM,
            transcendentals=requests * GROUP * positions,
        ),
    )(
        cache_length,
        adapter_table_row,
        request_adapter.reshape(1, requests),
        queries,
        token_keys,
        token_values,
        cached_key_rows,
        cached_value_rows,
    )


def down_kernel(*refs):
    routed, weights, out_ref = refs[:RING], refs[RING:-1], refs[-1]
    rank = weights[0].shape[0]
    features = routed[0].shape[1]
    pair = CORES * CAP
    for k in range(Z_CHIPS):
        rows = jnp.concatenate([r[k * pair : (k + 1) * pair, :] for r in routed], axis=0)
        products = [
            lax.dot_general(
                rows,
                w[:, :features],
                (((1,), (1,)), ((), ())),
                preferred_element_type=jnp.float32,
            )
            for w in weights[k * CORES : (k + 1) * CORES]
        ]
        for m in range(RING):
            at = (k * RING + m) * CAP
            for j, product in enumerate(products):
                row = m * pair + j * CAP
                out_ref[at : at + CAP, j * rank : (j + 1) * rank] = product[row : row + CAP, :]


def down(routed, weights):
    rank = weights[0].shape[0]
    vmem = pl.BlockSpec(memory_space=pltpu.VMEM)
    return pl.pallas_call(
        down_kernel,
        in_specs=[vmem] * (len(routed) + len(weights)),
        out_specs=vmem,
        out_shape=jax.ShapeDtypeStruct((Z_CHIPS * RING * CAP, CORES * rank), jnp.float32),
        compiler_params=pltpu.CompilerParams(vmem_limit_bytes=16 * 2**20),
    )(*routed, *weights)


def up_kernel(columns, *refs):
    partials, weights, deltas = refs[:RING], refs[RING:-RING], refs[-RING:]
    rank = weights[0].shape[0]
    pair = CORES * CAP
    total = partials[0][...] + partials[1][...] + partials[2][...] + partials[3][...]
    for k in range(Z_CHIPS):
        part = total[k * RING * CAP : (k + 1) * RING * CAP, :]
        spread = []
        for m in range(RING):
            spread += [part[m * CAP : (m + 1) * CAP, :]] * CORES
        spread = jnp.concatenate(spread, axis=0)
        row = lax.broadcasted_iota(jnp.int32, spread.shape, 0)
        lane = lax.broadcasted_iota(jnp.int32, spread.shape, 1)
        low_rank = jnp.where((row // CAP) % CORES == lane // rank, spread, 0.0)
        low_rank = low_rank.astype(jnp.bfloat16)
        delta = 0.0
        for j, w in enumerate(weights[k * CORES : (k + 1) * CORES]):
            delta += jnp.dot(
                low_rank[:, j * rank : (j + 1) * rank],
                w[:, w.shape[1] - columns :],
                preferred_element_type=jnp.float32,
            )
        delta = delta.astype(jnp.bfloat16)
        for m, delta_ref in enumerate(deltas):
            delta_ref[k * pair : (k + 1) * pair, :] = delta[m * pair : (m + 1) * pair, :]


def up(partials, weights, columns):
    rows = Z_CHIPS * CORES * CAP
    vmem = pl.BlockSpec(memory_space=pltpu.VMEM)
    return pl.pallas_call(
        functools.partial(up_kernel, columns),
        in_specs=[vmem] * (len(partials) + len(weights)),
        out_specs=[vmem] * RING,
        out_shape=[jax.ShapeDtypeStruct((rows, columns), jnp.bfloat16)] * RING,
        compiler_params=pltpu.CompilerParams(vmem_limit_bytes=16 * 2**20),
    )(*partials, *weights)


def project_kernel(piece_hbm, weight_hbm, out_ref, piece_ref, weight_ref, piece_sem, sem):
    depth = weight_ref.shape[0] // sem.shape[0]
    per_piece = piece_ref.shape[2] // depth

    def fetch(c):
        at = pl.ds(c * depth, depth)
        return pltpu.make_async_copy(weight_hbm.at[at], weight_ref.at[at], sem.at[c])

    pieces = pltpu.make_async_copy(piece_hbm, piece_ref, piece_sem)
    pieces.start()
    count = sem.shape[0]
    for c in range(min(PROJECT_AHEAD, count)):
        fetch(c).start()
    pieces.wait()
    for c in range(count):
        if c + PROJECT_AHEAD < count:
            fetch(c + PROJECT_AHEAD).start()
        fetch(c).wait()
        piece, part = c // per_piece, c % per_piece
        product = jnp.dot(
            piece_ref[piece, :, part * depth : (part + 1) * depth],
            weight_ref[c * depth : (c + 1) * depth, :],
            preferred_element_type=jnp.float32,
        )
        if c == 0:
            out_ref[...] = product
        else:
            out_ref[...] += product


def project(pieces, weights):
    count, requests, features = pieces.shape
    columns = weights.shape[1]
    hbm = pl.BlockSpec(memory_space=pltpu.HBM)
    return pl.pallas_call(
        project_kernel,
        in_specs=[hbm, hbm],
        out_specs=pl.BlockSpec(memory_space=pltpu.VMEM),
        out_shape=jax.ShapeDtypeStruct((requests, columns), jnp.float32),
        scratch_shapes=[
            pltpu.VMEM(pieces.shape, jnp.bfloat16),
            pltpu.VMEM(weights.shape, jnp.bfloat16),
            pltpu.SemaphoreType.DMA,
            pltpu.SemaphoreType.DMA((weights.shape[0] // DEPTH,)),
        ],
        compiler_params=pltpu.CompilerParams(vmem_limit_bytes=52 * 2**20),
        cost_estimate=pl.CostEstimate(
            flops=2 * count * requests * features * columns,
            bytes_accessed=2 * count * features * columns,
            transcendentals=0,
        ),
    )(pieces, weights)


def swap_tensor(value, k):
    return lax.ppermute(value, "tensor", [(i, i ^ k) for i in range(RING)])


def swap_dp(value, k):
    return lax.ppermute(value, "dp", [(i, i ^ k) for i in range(RING * Z_CHIPS * CORES)])


def swap_y(value, k):
    return swap_dp(value, k * Z_CHIPS * CORES)


def swap_z(value, k):
    return swap_dp(value, k * CORES)


def swap_core(value):
    return swap_dp(value, 1)


def on_device(
    queries,
    token_keys,
    token_values,
    cached_key_rows,
    cached_value_rows,
    cache_length,
    output_projection,
    request_adapter,
    adapter_table_row,
    adapter_down_weight,
    adapter_up_weight,
):
    bf16, f32 = jnp.bfloat16, jnp.float32
    requests = queries.shape[0]
    columns = output_projection.shape[1]
    owned = Z_CHIPS * CORES
    here = lax.axis_index("dp")

    down_here, up_here = adapter_down_weight[0], adapter_up_weight[0]
    both = jnp.concatenate([down_here, up_here], axis=1)
    beside = [swap_z(both, k) for k in (1, 3)]
    both_other = swap_core(both)

    attended, *placed = attend(
        queries,
        token_keys,
        token_values,
        cached_key_rows,
        cached_value_rows,
        cache_length,
        request_adapter,
        adapter_table_row,
        owned * CAP,
    )
    pieces = lax.all_to_all(attended, "tensor", 0, 0)
    placed, both_late, request_adapter = lax.optimization_barrier(
        (placed, both, request_adapter)
    )
    across = swap_z(both_late, 2)
    placed, beside, both_other = lax.optimization_barrier((placed, beside, both_other))
    beside_other = [swap_core(w) for w in beside]
    routed = [placed[0]] + [swap_y(placed[m], m) for m in range(1, RING)]
    routed, across = lax.optimization_barrier((routed, across))
    table = [both, both_other, beside[0], beside_other[0]]
    table += [across, swap_core(across), beside[1], beside_other[1]]

    every_adapter = adapter_table_row.shape[0]
    matches = request_adapter[:, None] == jnp.arange(every_adapter, dtype=jnp.int32)[None, :]
    slot_of = jnp.sum(jnp.where(matches, adapter_table_row[None, :], 0), axis=1)
    order = jnp.arange(requests, dtype=jnp.int32)
    earlier = (slot_of[:, None] == slot_of[None, :]) & (order[:, None] > order[None, :])
    position = (slot_of ^ here) * CAP + jnp.sum(earlier.astype(jnp.int32), axis=1)
    placing = (
        position[:, None] == jnp.arange(every_adapter * CAP, dtype=jnp.int32)[None, :]
    ).astype(bf16)

    partial = down(routed, table)
    partials = [partial] + [swap_tensor(partial, k) for k in range(1, RING)]
    partials, pieces = lax.optimization_barrier((partials, pieces))
    projected = project(pieces, output_projection)

    delta = up(partials, table, columns)
    back = [delta[0]] + [swap_y(delta[m], m) for m in range(1, RING)]
    returned = jnp.dot(placing, jnp.concatenate(back, axis=0), preferred_element_type=f32)
    return (projected + returned).astype(bf16)


def solution(mesh):
    in_specs = (
        P("dp", "tensor"),
        P("dp", "tensor"),
        P("dp", "tensor"),
        P("dp", None, "tensor"),
        P("dp", None, "tensor"),
        P("dp"),
        P(None, "tensor"),
        P("dp"),
        P(),
        P("dp", None, "tensor"),
        P("dp", None, "tensor"),
    )
    out_specs = P("dp", "tensor")
    return jax.shard_map(
        on_device, mesh=mesh, in_specs=in_specs, out_specs=out_specs, check_vma=False
    )
```
